32 devices in a mesh: ep: 8 (over z, y), tp: 4 (over x, core).
Axes of the slice: x: 2, y: 2, z: 4, core: 2. Of those that a mesh axis runs over, the one named last changes fastest.
Arguments:
- tokens: bfloat16 [1024, 2048], P('ep', 'tp'), may hold values from -6 to 6
- cotangent: bfloat16 [1024, 2048], P('ep', 'tp'), may hold values from -6 to 6
- token_expert: int32 [1024], P('ep'), may hold values from 0 to 7, as said below
- partner: int32 [8], replicated, may hold values from 0 to 7, as said below
- gate_weight: bfloat16 [8, 768, 2048], P('ep', 'tp'), may hold values from -0.125 to 0.125
- up_weight: bfloat16 [8, 768, 2048], P('ep', 'tp'), may hold values from -0.125 to 0.125
- down_weight: bfloat16 [8, 768, 2048], P('ep', 'tp'), may hold values from -0.21875 to 0.21875
Outputs:
- token_grad: bfloat16 [1024, 2048], P('ep', 'tp')
- gate_grad: bfloat16 [8, 768, 2048], P('ep', 'tp')
- up_grad: bfloat16 [8, 768, 2048], P('ep', 'tp')
- down_grad: bfloat16 [8, 768, 2048], P('ep', 'tp')
The draws below stay inside these ranges and needn't reach their ends.
Inputs may be any that keep to these rules, and one draw needn't show every extreme that they name: partner[partner[d]] = d and partner[d] != d: the devices of ep swap their experts in pairs. `token_expert`: each aligned block of 128 rows (the rows of one device) names each expert at most 32 times, and one expert, the same for all blocks, exactly 32 times in every block.
All inputs are finite; a program needn't handle non-finite values.
Results may differ from the reference program's by a relative error of at most 0.0049.
Values may be sent and summed in bfloat16 or wider, within the bound.
A program may use at most 64 MiB of HBM per device.

```python
import jax
import jax.numpy as jnp
from jax import lax

D = 2048
F = 768
TOK_DEV = 128
EXPERTS = 8
CAP = 32
ROWS = 1024
N_EP = 8


def draw_partner(key, part):
    shuffled = jax.random.permutation(key, EXPERTS).astype(jnp.int32)
    paired = shuffled.reshape(-1, 2)[:, ::-1].reshape(-1)
    return jnp.zeros((EXPERTS,), jnp.int32).at[shuffled].set(paired)


def draw_token_expert(key, part):
    hottest = jax.random.randint(jax.random.fold_in(key, 7), (), 0, EXPERTS).astype(jnp.int32)

    def one_block(block_index):
        sub_key = jax.random.fold_in(key, block_index)
        scores = jax.random.permutation(jax.random.fold_in(sub_key, 1), EXPERTS * CAP).astype(jnp.int32)
        slot_ids = jnp.arange(EXPERTS * CAP, dtype=jnp.int32)
        owners = slot_ids // CAP
        scores = jnp.where(owners == hottest, slot_ids % CAP - CAP, scores)
        chosen = owners[jnp.argsort(scores, stable=True)][:TOK_DEV]
        return chosen[jax.random.permutation(jax.random.fold_in(sub_key, 2), TOK_DEV)]
    return jax.vmap(one_block)(jnp.arange(N_EP, dtype=jnp.int32)).reshape(-1).astype(jnp.int32)


def block_scale(key, extent, pieces, low, largest):
    loudness, own = 1.0, jax.random.fold_in(key, 6)
    for dim, shards_of in pieces:
        draws = jnp.exp(jax.random.uniform(jax.random.fold_in(own, dim), (shards_of,), jnp.float32, low / len(pieces), largest / len(pieces)))
        loudness = loudness * jnp.repeat(draws, extent[dim] // shards_of).reshape([-1 if axis == dim else 1 for axis in range(len(extent))])
    return loudness


def gaussian(stream_key, shape, scale, reach, split=(), kind=jnp.bfloat16):
    array = jax.random.normal(stream_key, shape, jnp.float32) * scale
    if len(split) > 0:
        array = block_scale(stream_key, shape, split, -0.22, 0.18) * array
    return jnp.clip(array, min=-reach, max=reach).astype(kind)


def setup_inputs(seed: int = 0) -> dict:
    arg_keys = jax.random.split(jax.random.key(seed), 8)
    tokens = gaussian(arg_keys[0], (ROWS, D), 1.0, 6.0, ((0, 8), (1, 4)))
    cotangent = gaussian(arg_keys[1], (ROWS, D), 1.0, 6.0, ((0, 8), (1, 4)))
    token_expert = draw_token_expert(jax.random.fold_in(arg_keys[7], 71), 0)
    partner = draw_partner(jax.random.fold_in(arg_keys[7], 71), 0)
    gate_weight = gaussian(arg_keys[4], (EXPERTS, F, D), D ** -0.5, 0.125, ((0, 8), (1, 4)))
    up_weight = gaussian(arg_keys[5], (EXPERTS, F, D), D ** -0.5, 0.125, ((0, 8), (1, 4)))
    down_weight = gaussian(arg_keys[6], (EXPERTS, F, D), F ** -0.5, 0.21875, ((0, 8), (1, 4)))
    return dict(tokens=tokens, cotangent=cotangent, token_expert=token_expert, partner=partner, gate_weight=gate_weight, up_weight=up_weight, down_weight=down_weight)


def expert_math(full_x, full_g, w_gate, w_up, w_down):
    gate = jnp.dot(full_x, w_gate.T, preferred_element_type=jnp.float32)
    upward = jnp.dot(full_x, w_up.T, preferred_element_type=jnp.float32)
    sigmoid_gate = jax.nn.sigmoid(gate)
    activated = gate * sigmoid_gate
    hidden = (activated * upward).astype(jnp.bfloat16)
    hidden_grad = jnp.dot(full_g, w_down.T, preferred_element_type=jnp.float32)
    up_term = (hidden_grad * activated).astype(jnp.bfloat16)
    gate_term = (hidden_grad * upward * sigmoid_gate * (1.0 + gate * (1.0 - sigmoid_gate))).astype(jnp.bfloat16)
    row_grad = jnp.dot(gate_term, w_gate, preferred_element_type=jnp.float32) + jnp.dot(up_term, w_up, preferred_element_type=jnp.float32)
    grad_gate = jnp.dot(gate_term.T, full_x, preferred_element_type=jnp.float32).astype(jnp.bfloat16)
    grad_up = jnp.dot(up_term.T, full_x, preferred_element_type=jnp.float32).astype(jnp.bfloat16)
    grad_down = jnp.dot(hidden.T, full_g, preferred_element_type=jnp.float32).astype(jnp.bfloat16)
    return row_grad.astype(jnp.bfloat16), grad_gate, grad_up, grad_down


def reference(tokens, cotangent, token_expert, partner, gate_weight, up_weight, down_weight):
    capacity = N_EP * CAP
    row_total = tokens.shape[0]
    owners = token_expert.astype(jnp.int32)
    sorted_rows = jnp.argsort(owners, stable=True).astype(jnp.int32)
    counts = jnp.sum((owners[None, :] == jnp.arange(EXPERTS, dtype=jnp.int32)[:, None]).astype(jnp.int32), axis=1)
    starts = (jnp.cumsum(counts) - counts).astype(jnp.int32)
    offsets = jnp.arange(capacity, dtype=jnp.int32)
    picked = jnp.take(sorted_rows, jnp.minimum(starts[:, None] + offsets[None, :], row_total - 1))
    picked = jnp.where(offsets[None, :] < counts[:, None], picked, row_total).astype(jnp.int32)
    padded_x = jnp.concatenate([tokens, jnp.zeros((1, D), jnp.bfloat16)], axis=0)
    padded_g = jnp.concatenate([cotangent, jnp.zeros((1, D), jnp.bfloat16)], axis=0)

    def expert_step(inputs):
        rows_of, w_gate, w_up, w_down = inputs
        return expert_math(padded_x[rows_of], padded_g[rows_of], w_gate, w_up, w_down)

    row_grads, grad_gate, grad_up, grad_down = lax.map(expert_step, (picked, gate_weight, up_weight, down_weight))
    token_grad = jnp.zeros((row_total + 1, D), jnp.bfloat16).at[picked.reshape(-1)].set(row_grads.reshape(-1, D))[:row_total]
    gate_grad = jnp.take(grad_gate, partner.astype(jnp.int32), axis=0)
    up_grad = jnp.take(grad_up, partner.astype(jnp.int32), axis=0)
    down_grad = jnp.take(grad_down, partner.astype(jnp.int32), axis=0)
    return token_grad, gate_grad, up_grad, down_grad
```

```python
import functools

import jax
import jax.numpy as jnp
from jax import lax
from jax.experimental import pallas as pl
from jax.experimental.pallas import tpu as pltpu
from jax.sharding import PartitionSpec as P

F32 = jnp.float32
BF16 = jnp.bfloat16


def contract_last(left, right):
    return lax.dot_general(left, right, (((1,), (1,)), ((), ())), preferred_element_type=F32)


def contract_first(left, right):
    return lax.dot_general(left, right, (((0,), (0,)), ((), ())), preferred_element_type=F32)


def expert_terms(gate, upward, hidden_grad):
    sigmoid_gate = jax.nn.sigmoid(gate)
    activated = gate * sigmoid_gate
    hidden = (activated * upward).astype(BF16)
    up_term = (hidden_grad * activated).astype(BF16)
    gate_term = (hidden_grad * upward * sigmoid_gate * (1.0 + gate * (1.0 - sigmoid_gate))).astype(BF16)
    return gate_term, up_term, hidden


def capacity_of(rows, devices):
    return max(2, (2 * rows + devices - 1) // devices)


def relocate(arrays, partner):
    devices = lax.axis_size("ep")
    pieces = tuple((matrix.reshape(devices, -1) for matrix in arrays))
    spread = lax.all_to_all(pieces, "ep", split_axis=0, concat_axis=0, tiled=True)
    chosen = tuple((jnp.take(piece, partner, axis=0) for piece in spread))
    returned = lax.all_to_all(chosen, "ep", split_axis=0, concat_axis=0, tiled=True)
    return tuple((piece.reshape(matrix.shape) for piece, matrix in zip(returned, arrays)))


def plain_body(tokens, cotangent, token_expert, partner, gate_weight, up_weight, down_weight):
    devices = lax.axis_size("ep")
    row_count = tokens.shape[0]
    capacity = capacity_of(row_count, devices)
    gate_weight, up_weight, down_weight = relocate((gate_weight, up_weight, down_weight), partner)
    owners = jnp.take(partner, token_expert, axis=0)
    same_owner = owners[:, None] == owners[None, :]
    earlier = jnp.arange(row_count)[:, None] > jnp.arange(row_count)[None, :]
    position = jnp.sum((same_owner & earlier).astype(jnp.int32), axis=1)
    slot_of = owners * capacity + position
    one_hot = (slot_of[None, :] == jnp.arange(devices * capacity)[:, None]).astype(BF16)
    send_x = jnp.dot(one_hot, tokens, preferred_element_type=F32).astype(BF16)
    send_g = jnp.dot(one_hot, cotangent, preferred_element_type=F32).astype(BF16)
    received_x = lax.all_to_all(send_x, "ep", split_axis=0, concat_axis=0, tiled=True)
    received_g = lax.all_to_all(send_g, "ep", split_axis=0, concat_axis=0, tiled=True)
    full_x = lax.all_gather(received_x, "tp", axis=1, tiled=True)
    full_g = lax.all_gather(received_g, "tp", axis=1, tiled=True)
    w_gate, w_up, w_down = gate_weight[0], up_weight[0], down_weight[0]
    gate_term, up_term, hidden = expert_terms(
        contract_last(full_x, w_gate), contract_last(full_x, w_up), contract_last(full_g, w_down)
    )
    partial_value = jnp.dot(gate_term, w_gate, preferred_element_type=F32) + jnp.dot(
        up_term, w_up, preferred_element_type=F32
    )
    grad_gate = contract_first(gate_term, full_x).astype(BF16)[None]
    grad_up = contract_first(up_term, full_x).astype(BF16)[None]
    grad_down = contract_first(hidden, full_g).astype(BF16)[None]
    share = lax.psum_scatter(partial_value, "tp", scatter_dimension=1, tiled=True).astype(BF16)
    coming_back = lax.all_to_all(share, "ep", split_axis=0, concat_axis=0, tiled=True)
    token_grad = contract_first(one_hot, coming_back).astype(BF16)
    return (token_grad, grad_gate, grad_up, grad_down)


def remote(src, dst, send, recv, device):
    return pltpu.make_async_remote_copy(
        src_ref=src, dst_ref=dst, send_sem=send, recv_sem=recv,
        device_id=device, device_id_type=pl.DeviceIdType.MESH,
    )


def swap_kernel(
    n, cap, groups,
    partner, te, tok, cot, wg_in, wu_in, wd_in,
    tg_out, gg_out, gu_out, gd_out,
    w_v, send_e, send_p, full_e, full_p, terms, mid, send2, terms_p,
    keep, c1s, c1r, c2s, c2r, shares, ret,
    w_sem, ae, ap, be, bp, e1, e2, c1, c2, dd,
):
    rows, width = tok.shape
    units = wg_in.shape[1]
    per = n // groups
    me = lax.axis_index("ep")
    t = lax.axis_index("tp")
    sib = t + 1 - 2 * lax.rem(t, 2)
    ctr = lax.rem(t + 2, 4)
    far = lax.rem(sib + 2, 4)
    ahead = lambda k: lax.rem(me + k, n)
    behind = lambda k: lax.rem(me + n - k, n)

    barrier = pltpu.get_barrier_semaphore()

    def greet(k, carry):
        pl.semaphore_signal(barrier, inc=1, device_id={"ep": ahead(k)}, device_id_type=pl.DeviceIdType.MESH)
        return carry

    lax.fori_loop(1, n, greet, 0)
    for other in (sib, ctr):
        pl.semaphore_signal(barrier, inc=1, device_id={"tp": other}, device_id_type=pl.DeviceIdType.MESH)

    w_copies = [
        pltpu.make_async_copy(
            w.at[0, :, pl.ds(q * width, width)], w_v.at[i, q], w_sem.at[i, q]
        )
        for i, w in enumerate((wg_in, wu_in, wd_in))
        for q in range(4)
    ]
    for copy in w_copies:
        copy.start()

    te_lane = jnp.broadcast_to(te[...].astype(F32), (rows, rows))
    te_sub = te_lane.T
    at0 = lax.broadcasted_iota(jnp.int32, (rows, rows), 0)
    at1 = lax.broadcasted_iota(jnp.int32, (rows, rows), 1)
    same = te_lane == te_sub
    pos_lane = jnp.sum(jnp.where(same & (at0 < at1), 1.0, 0.0), axis=0, keepdims=True)
    pos_sub = jnp.sum(jnp.where(same & (at1 < at0), 1.0, 0.0), axis=1, keepdims=True)
    slot_lane = te[...].astype(F32) * float(cap) + pos_lane
    slot_sub = te_sub[:, :1] * float(cap) + pos_sub
    slots = n * cap
    down = lax.broadcasted_iota(jnp.int32, (slots, rows), 0).astype(F32)
    across = lax.broadcasted_iota(jnp.int32, (rows, slots), 1).astype(F32)

    def pick(slot, send):
        hot = jnp.where(down == slot, 1.0, 0.0).astype(BF16)
        for i, source in enumerate((tok, cot)):
            rows_of = jnp.dot(hot, source[...], preferred_element_type=F32).astype(BF16)
            send[:, i] = rows_of.reshape(n, cap, width)

    def dispatch(send, full, sem):
        def go(k, carry):
            to = ahead(k)
            remote(send.at[to], full.at[t, me], sem.at[0, to], sem.at[1, me], {"ep": to}).start()
            return carry
        lax.fori_loop(1, n, go, 0)
        full[t, me] = send[me]

    def share_own(full, b, s):
        remote(full.at[t, s], full.at[t, s], b.at[1, s], b.at[4, s], {"tp": ctr}).start()
        remote(full.at[t, s], full.at[t, s], b.at[0, s], b.at[3, s], {"tp": sib}).start()

    def got_own(full, a, s, k):
        remote(full.at[t, s], full.at[t, s], a.at[0, s], a.at[1, s], {"ep": s}).wait_recv()

    def pass_on(full, b, s):
        remote(full.at[ctr, s], full.at[ctr, s], b.at[1, s], b.at[4, s], {"tp": ctr}).wait_recv()
        remote(full.at[ctr, s], full.at[ctr, s], b.at[2, s], b.at[5, s], {"tp": sib}).start()

    def got_sibling(full, b, s):
        remote(full.at[sib, s], full.at[sib, s], b.at[0, s], b.at[3, s], {"tp": sib}).wait_recv()
        remote(full.at[far, s], full.at[far, s], b.at[2, s], b.at[5, s], {"tp": sib}).wait_recv()

    def spread(full, a, b):
        share_own(full, b, me)

        def step(k, carry):
            s = behind(k)
            got_own(full, a, s, k)
            share_own(full, b, s)
            pass_on(full, b, behind(k - 1))
            return carry
        lax.fori_loop(1, n, step, 0)
        pass_on(full, b, behind(n - 1))

    pick(slot_lane, send_e)
    pl.semaphore_wait(barrier, n + 1)
    dispatch(send_e, full_e, ae)
    moved = pos_lane
    for e in range(n):
        moved = moved + jnp.where(te[...] == e, (partner[e] * cap).astype(F32), 0.0)
    pick(moved, send_p)
    spread(full_e, ae, be)
    dispatch(send_p, full_p, ap)
    for copy in w_copies:
        copy.wait()

    slices = (t, ctr, sib, far)
    for h in range(groups):
        ks = range(h * per, (h + 1) * per)
        for k in ks:
            got_sibling(full_e, be, behind(k))
        gate = jnp.zeros((per * cap, units), F32)
        upward = jnp.zeros((per * cap, units), F32)
        hidden_grad = jnp.zeros((per * cap, units), F32)
        for q in range(4):
            x_q = jnp.concatenate([full_e[q, behind(k), 0] for k in ks], axis=0)
            g_q = jnp.concatenate([full_e[q, behind(k), 1] for k in ks], axis=0)
            gate = gate + contract_last(x_q, w_v[0, q])
            upward = upward + contract_last(x_q, w_v[1, q])
            hidden_grad = hidden_grad + contract_last(g_q, w_v[2, q])
        gate_term, up_term, hidden = expert_terms(gate, upward, hidden_grad)
        for j, k in enumerate(ks):
            cut = slice(j * cap, (j + 1) * cap)
            terms[behind(k), :, 0:units] = gate_term[cut]
            terms[behind(k), :, units : 2 * units] = up_term[cut]
            terms[behind(k), :, 2 * units : 3 * units] = hidden[cut]
            if terms.shape[2] > 3 * units:
                terms[behind(k), :, 3 * units :] = jnp.zeros((cap, terms.shape[2] - 3 * units), BF16)
        for i in (2, 3):
            q = slices[i]
            c1s[h, i - 2] = (
                jnp.dot(gate_term, w_v[0, q], preferred_element_type=F32)
                + jnp.dot(up_term, w_v[1, q], preferred_element_type=F32)
            ).astype(BF16)
        remote(c1s.at[h], c1r.at[h], c1.at[0, h], c1.at[1, h], {"tp": sib}).start()
        for k in ks:
            s = behind(k)
            if k == 0:
                mid[me] = terms[me]
            else:
                remote(terms.at[s], mid.at[me], e1.at[0, s], e1.at[1, me], {"ep": s}).start()
        for i in (0, 1):
            q = slices[i]
            keep[h, i] = jnp.dot(gate_term, w_v[0, q], preferred_element_type=F32) + jnp.dot(
                up_term, w_v[1, q], preferred_element_type=F32
            )

    for h in range(groups):
        remote(c1s.at[h], c1r.at[h], c1.at[0, h], c1.at[1, h], {"tp": sib}).wait_recv()
        c2s[h] = (keep[h, 1] + c1r[h, 1].astype(F32)).astype(BF16)
        remote(c2s.at[h], c2r.at[h], c2.at[0, h], c2.at[1, h], {"tp": ctr}).start()

    def first_hop(k, carry):
        s = ahead(k)
        remote(mid.at[s], mid.at[s], e1.at[0, s], e1.at[1, s], {"ep": s}).wait_recv()
        return carry
    lax.fori_loop(1, n, first_hop, 0)

    for h in range(groups):
        remote(c2s.at[h], c2r.at[h], c2.at[0, h], c2.at[1, h], {"tp": ctr}).wait_recv()
        total = (keep[h, 0] + c1r[h, 0].astype(F32) + c2r[h].astype(F32)).astype(BF16)
        shares[h * per : (h + 1) * per] = total.reshape(per, cap, width)
        for k in range(h * per, (h + 1) * per):
            s = behind(k)
            if k == 0:
                ret[me] = shares[0]
            else:
                remote(shares.at[k], ret.at[me], dd.at[0, s], dd.at[1, me], {"ep": s}).start()

    def second_hop(k, carry):
        d = ahead(k)
        send2[d] = mid[partner[d]]
        remote(send2.at[d], terms_p.at[me], e2.at[0, d], e2.at[1, me], {"ep": d}).start()
        return carry
    lax.fori_loop(1, n, second_hop, 0)
    terms_p[me] = mid[partner[me]]

    spread(full_p, ap, bp)

    def returned(k, carry):
        s = behind(k)
        remote(ret.at[s], ret.at[s], dd.at[0, s], dd.at[1, s], {"ep": s}).wait_recv()
        return carry
    lax.fori_loop(1, n, returned, 0)
    home = jnp.where(across == slot_sub, 1.0, 0.0).astype(BF16)
    tg_out[...] = jnp.dot(home, ret[...].reshape(slots, width), preferred_element_type=F32).astype(BF16)

    def arrived(k, carry):
        s = behind(k)
        remote(terms_p.at[s], terms_p.at[s], e2.at[0, s], e2.at[1, s], {"ep": s}).wait_recv()
        return carry
    lax.fori_loop(1, n, arrived, 0)

    def gathered(k, carry):
        got_sibling(full_p, bp, behind(k))
        return carry
    lax.fori_loop(0, n, gathered, 0)

    flat = terms_p[...].reshape(slots, terms_p.shape[2])
    turned = flat.astype(F32).T.astype(BF16)
    for q in range(4):
        columns = slice(q * width, (q + 1) * width)
        x_q = full_p[q, :, 0].reshape(slots, width)
        g_q = full_p[q, :, 1].reshape(slots, width)
        gg_out[0, :, columns] = jnp.dot(turned[:units], x_q, preferred_element_type=F32).astype(BF16)
        gu_out[0, :, columns] = jnp.dot(turned[units : 2 * units], x_q, preferred_element_type=F32).astype(BF16)
        gd_out[0, :, columns] = jnp.dot(turned[2 * units : 3 * units], g_q, preferred_element_type=F32).astype(BF16)

    def drain(k, carry):
        s = ahead(k)
        remote(send_e.at[s], send_e.at[s], ae.at[0, s], ae.at[1, s], {"ep": s}).wait_send()
        remote(send_p.at[s], send_p.at[s], ap.at[0, s], ap.at[1, s], {"ep": s}).wait_send()
        remote(terms.at[s], terms.at[s], e1.at[0, s], e1.at[1, s], {"ep": s}).wait_send()
        remote(send2.at[s], send2.at[s], e2.at[0, s], e2.at[1, s], {"ep": s}).wait_send()
        remote(ret.at[s], ret.at[s], dd.at[0, s], dd.at[1, s], {"ep": s}).wait_send()
        return carry
    lax.fori_loop(1, n, drain, 0)

    def drain_tp(s, carry):
        for full, b in ((full_e, be), (full_p, bp)):
            for i, (q, other) in enumerate(((t, sib), (t, ctr), (ctr, sib))):
                remote(full.at[q, s], full.at[q, s], b.at[i, s], b.at[3 + i, s], {"tp": other}).wait_send()
        return carry
    lax.fori_loop(0, n, drain_tp, 0)
    for h in range(groups):
        remote(c1s.at[h], c1r.at[h], c1.at[0, h], c1.at[1, h], {"tp": sib}).wait_send()
        remote(c2s.at[h], c2r.at[h], c2.at[0, h], c2.at[1, h], {"tp": ctr}).wait_send()


def kernel_body(tokens, cotangent, token_expert, partner, gate_weight, up_weight, down_weight):
    n = lax.axis_size("ep")
    rows, width = tokens.shape
    _, units, features = gate_weight.shape
    cap = capacity_of(rows, n)
    groups = 2
    per = n // groups
    padded = -(-3 * units // 128) * 128
    dma = pltpu.SemaphoreType.DMA
    vmem = pl.BlockSpec(memory_space=pltpu.VMEM)
    anywhere = pl.BlockSpec(memory_space=pl.ANY)
    grad = jax.ShapeDtypeStruct((1, units, features), BF16)
    return pl.pallas_call(
        functools.partial(swap_kernel, n, cap, groups),
        out_shape=(jax.ShapeDtypeStruct((rows, width), BF16), grad, grad, grad),
        in_specs=[pl.BlockSpec(memory_space=pltpu.SMEM), vmem, vmem, vmem, anywhere, anywhere, anywhere],
        out_specs=(vmem, vmem, vmem, vmem),
        scratch_shapes=[
            pltpu.VMEM((3, 4, units, width), BF16),
            pltpu.VMEM((n, 2, cap, width), BF16),
            pltpu.VMEM((n, 2, cap, width), BF16),
            pltpu.VMEM((4, n, 2, cap, width), BF16),
            pltpu.VMEM((4, n, 2, cap, width), BF16),
            pltpu.VMEM((n, cap, padded), BF16),
            pltpu.VMEM((n, cap, padded), BF16),
            pltpu.VMEM((n, cap, padded), BF16),
            pltpu.VMEM((n, cap, padded), BF16),
            pltpu.VMEM((groups, 2, per * cap, width), F32),
            pltpu.VMEM((groups, 2, per * cap, width), BF16),
            pltpu.VMEM((groups, 2, per * cap, width), BF16),
            pltpu.VMEM((groups, per * cap, width), BF16),
            pltpu.VMEM((groups, per * cap, width), BF16),
            pltpu.VMEM((n, cap, width), BF16),
            pltpu.VMEM((n, cap, width), BF16),
            dma((3, 4)),
            dma((2, n)),
            dma((2, n)),
            dma((6, n)),
            dma((6, n)),
            dma((2, n)),
            dma((2, n)),
            dma((2, groups)),
            dma((2, groups)),
            dma((2, n)),
        ],
        compiler_params=pltpu.CompilerParams(
            collective_id=0, has_side_effects=True, vmem_limit_bytes=48 * 2**20
        ),
        cost_estimate=pl.CostEstimate(
            flops=16 * n * cap * units * features,
            bytes_accessed=12 * units * features + 6 * rows * width,
            transcendentals=n * cap * units,
        ),
    )(partner, token_expert.reshape(1, rows), tokens, cotangent, gate_weight, up_weight, down_weight)


def body(tokens, cotangent, token_expert, partner, gate_weight, up_weight, down_weight):
    n, ranks = lax.axis_size("ep"), lax.axis_size("tp")
    rows, width = tokens.shape
    cap = capacity_of(rows, n)
    tiled = cap % 16 == 0 and rows % 128 == 0 and width % 128 == 0 and n % 2 == 0 and ranks == 4
    fits = 32 * n * cap * width <= 8 * 2**20
    chosen = kernel_body if tiled and fits else plain_body
    return chosen(tokens, cotangent, token_expert, partner, gate_weight, up_weight, down_weight)


def solution(mesh):
    in_specs = (
        P("ep", "tp"),
        P("ep", "tp"),
        P("ep"),
        P(),
        P("ep", "tp", None),
        P("ep", "tp", None),
        P("ep", "tp", None),
    )
    out_specs = (P("ep", "tp"), P("ep", "tp", None), P("ep", "tp", None), P("ep", "tp", None))
    return jax.shard_map(body, mesh=mesh, in_specs=in_specs, out_specs=out_specs, check_vma=False)
```

```python
import functools

import jax
import jax.numpy as jnp
from jax import lax
from jax.experimental import pallas as pl
from jax.experimental.pallas import tpu as pltpu
from jax.sharding import PartitionSpec as P

F32 = jnp.float32
BF16 = jnp.bfloat16


def contract_last(left, right):
    return lax.dot_general(left, right, (((1,), (1,)), ((), ())), preferred_element_type=F32)


def contract_first(left, right):
    return lax.dot_general(left, right, (((0,), (0,)), ((), ())), preferred_element_type=F32)


def expert_terms(gate, upward, hidden_grad):
    sigmoid_gate = jax.nn.sigmoid(gate)
    activated = gate * sigmoid_gate
    hidden = (activated * upward).astype(BF16)
    up_term = (hidden_grad * activated).astype(BF16)
    gate_term = (hidden_grad * upward * sigmoid_gate * (1.0 + gate * (1.0 - sigmoid_gate))).astype(BF16)
    return gate_term, up_term, hidden


def capacity_of(rows, devices):
    return max(2, (2 * rows + devices - 1) // devices)


def relocate(arrays, partner):
    devices = lax.axis_size("ep")
    pieces = tuple((matrix.reshape(devices, -1) for matrix in arrays))
    spread = lax.all_to_all(pieces, "ep", split_axis=0, concat_axis=0, tiled=True)
    chosen = tuple((jnp.take(piece, partner, axis=0) for piece in spread))
    returned = lax.all_to_all(chosen, "ep", split_axis=0, concat_axis=0, tiled=True)
    return tuple((piece.reshape(matrix.shape) for piece, matrix in zip(returned, arrays)))


def plain_body(tokens, cotangent, token_expert, partner, gate_weight, up_weight, down_weight):
    devices = lax.axis_size("ep")
    row_count = tokens.shape[0]
    capacity = capacity_of(row_count, devices)
    gate_weight, up_weight, down_weight = relocate((gate_weight, up_weight, down_weight), partner)
    owners = jnp.take(partner, token_expert, axis=0)
    same_owner = owners[:, None] == owners[None, :]
    earlier = jnp.arange(row_count)[:, None] > jnp.arange(row_count)[None, :]
    position = jnp.sum((same_owner & earlier).astype(jnp.int32), axis=1)
    slot_of = owners * capacity + position
    one_hot = (slot_of[None, :] == jnp.arange(devices * capacity)[:, None]).astype(BF16)
    send_x = jnp.dot(one_hot, tokens, preferred_element_type=F32).astype(BF16)
    send_g = jnp.dot(one_hot, cotangent, preferred_element_type=F32).astype(BF16)
    received_x = lax.all_to_all(send_x, "ep", split_axis=0, concat_axis=0, tiled=True)
    received_g = lax.all_to_all(send_g, "ep", split_axis=0, concat_axis=0, tiled=True)
    full_x = lax.all_gather(received_x, "tp", axis=1, tiled=True)
    full_g = lax.all_gather(received_g, "tp", axis=1, tiled=True)
    w_gate, w_up, w_down = gate_weight[0], up_weight[0], down_weight[0]
    gate_term, up_term, hidden = expert_terms(
        contract_last(full_x, w_gate), contract_last(full_x, w_up), contract_last(full_g, w_down)
    )
    partial_value = jnp.dot(gate_term, w_gate, preferred_element_type=F32) + jnp.dot(
        up_term, w_up, preferred_element_type=F32
    )
    grad_gate = contract_first(gate_term, full_x).astype(BF16)[None]
    grad_up = contract_first(up_term, full_x).astype(BF16)[None]
    grad_down = contract_first(hidden, full_g).astype(BF16)[None]
    share = lax.psum_scatter(partial_value, "tp", scatter_dimension=1, tiled=True).astype(BF16)
    coming_back = lax.all_to_all(share, "ep", split_axis=0, concat_axis=0, tiled=True)
    token_grad = contract_first(one_hot, coming_back).astype(BF16)
    return (token_grad, grad_gate, grad_up, grad_down)


def remote(src, dst, send, recv, device):
    return pltpu.make_async_remote_copy(
        src_ref=src, dst_ref=dst, send_sem=send, recv_sem=recv,
        device_id=device, device_id_type=pl.DeviceIdType.MESH,
    )


def slots_of(te, cap):
    rows = te.shape[1]
    te_lane = jnp.broadcast_to(te.astype(F32), (rows, rows))
    te_sub = te_lane.T
    at0 = lax.broadcasted_iota(jnp.int32, (rows, rows), 0)
    at1 = lax.broadcasted_iota(jnp.int32, (rows, rows), 1)
    same = te_lane == te_sub
    pos_lane = jnp.sum(jnp.where(same & (at0 < at1), 1.0, 0.0), axis=0, keepdims=True)
    pos_sub = jnp.sum(jnp.where(same & (at1 < at0), 1.0, 0.0), axis=1, keepdims=True)
    return te.astype(F32) * float(cap) + pos_lane, pos_lane, te_sub[:, :1] * float(cap) + pos_sub


WAVE, G0, BP = False, 0, 0


def result_kernel(
    cap, te, full_p, terms_p, ret, tg_out, gg_out, gu_out, gd_out, tg_v, g_v, out_sem
):
    n, _, padded = terms_p.shape
    rows, width = tg_v.shape
    units = g_v.shape[1]
    slots = n * cap
    turned = terms_p[...].reshape(slots, padded).astype(F32).T.astype(BF16)
    copies = []
    for q in range(4):
        columns = pl.ds(q * width, width)
        x_q = full_p[q, :, 0].reshape(slots, width)
        g_q = full_p[q, :, 1].reshape(slots, width)
        for i, (out, by) in enumerate(((gg_out, x_q), (gu_out, x_q), (gd_out, g_q))):
            part = turned[i * units : (i + 1) * units]
            g_v[3 * q + i] = jnp.dot(part, by, preferred_element_type=F32).astype(BF16)
            copy = pltpu.make_async_copy(g_v.at[3 * q + i], out.at[0, :, columns], out_sem.at[3 * q + i])
            copy.start()
            copies.append(copy)
    _, _, slot_sub = slots_of(te[...], cap)
    across = lax.broadcasted_iota(jnp.int32, (rows, slots), 1).astype(F32)
    home = jnp.where(across == slot_sub, 1.0, 0.0).astype(BF16)
    tg_v[...] = jnp.dot(home, ret[...].reshape(slots, width), preferred_element_type=F32).astype(BF16)
    copy = pltpu.make_async_copy(tg_v, tg_out, out_sem.at[12])
    copy.start()
    for done in copies + [copy]:
        done.wait()


def swap_kernel(
    n, cap, groups,
    partner, te, tok_in, cot_in, wg_in, wu_in, wd_in,
    full_p, terms_p, ret,
    tok, cot, w_v, send_e, send_p, full_e, terms, mid, send2,
    keep, c1s, c1r, c2s, c2r, shares,
    t_sem, w_sem, ae, ap, be, bp, e1, e2, c1, c2, dd,
):
    rows, width = tok.shape
    units = wg_in.shape[1]
    per = n // groups
    me = lax.axis_index("ep")
    t = lax.axis_index("tp")
    sib = t + 1 - 2 * lax.rem(t, 2)
    ctr = lax.rem(t + 2, 4)
    far = lax.rem(sib + 2, 4)
    order = [i + j for i in range(n // 2) for j in (0, n // 2)]
    ahead = lambda k: lax.rem(me + k, n)
    behind = lambda k: lax.rem(me + n - k, n)

    t_copies = [
        pltpu.make_async_copy(a, v, t_sem.at[i]) for i, (a, v) in enumerate(((tok_in, tok), (cot_in, cot)))
    ]
    for copy in t_copies:
        copy.start()
    barrier = pltpu.get_barrier_semaphore()

    def greet(k, carry):
        pl.semaphore_signal(barrier, inc=1, device_id={"ep": ahead(k)}, device_id_type=pl.DeviceIdType.MESH)
        return carry

    lax.fori_loop(1, n, greet, 0)
    for other in (sib, ctr):
        pl.semaphore_signal(barrier, inc=1, device_id={"tp": other}, device_id_type=pl.DeviceIdType.MESH)

    w_copies = [
        pltpu.make_async_copy(
            w.at[0, :, pl.ds(q * width, width)], w_v.at[i, q], w_sem.at[i, q]
        )
        for i, w in enumerate((wg_in, wu_in, wd_in))
        for q in range(4)
    ]
    for copy in w_copies:
        copy.start()

    slot_lane, pos_lane, _ = slots_of(te[...], cap)
    slots = n * cap
    down = lax.broadcasted_iota(jnp.int32, (slots, rows), 0).astype(F32)

    def pick(slot, send):
        hot = jnp.where(down == slot, 1.0, 0.0).astype(BF16)
        for i, source in enumerate((tok, cot)):
            rows_of = jnp.dot(hot, source[...], preferred_element_type=F32).astype(BF16)
            send[:, i] = rows_of.reshape(n, cap, width)

    def dispatch(send, full, sem, ks):
        for k in ks:
            to = ahead(k)
            remote(send.at[to], full.at[t, me], sem.at[0, to], sem.at[1, me], {"ep": to}).start()

    def sent(send, sem, ks):
        for k in ks:
            to = ahead(k)
            remote(send.at[to], send.at[to], sem.at[0, to], sem.at[1, to], {"ep": to}).wait_send()

    def share_own(full, b, s):
        remote(full.at[t, s], full.at[t, s], b.at[1, s], b.at[4, s], {"tp": ctr}).start()
        remote(full.at[t, s], full.at[t, s], b.at[0, s], b.at[3, s], {"tp": sib}).start()

    def got_own(full, a, s, k):
        remote(full.at[t, s], full.at[t, s], a.at[0, s], a.at[1, s], {"ep": s}).wait_recv()

    def pass_on(full, b, s):
        remote(full.at[ctr, s], full.at[ctr, s], b.at[1, s], b.at[4, s], {"tp": ctr}).wait_recv()
        remote(full.at[ctr, s], full.at[ctr, s], b.at[2, s], b.at[5, s], {"tp": sib}).start()

    def got_sibling(full, b, s):
        remote(full.at[sib, s], full.at[sib, s], b.at[0, s], b.at[3, s], {"tp": sib}).wait_recv()
        remote(full.at[far, s], full.at[far, s], b.at[2, s], b.at[5, s], {"tp": sib}).wait_recv()

    def take(full, a, b, ks):
        for k in ks:
            s = behind(k)
            if k:
                got_own(full, a, s, k)
            share_own(full, b, s)

    def relay(full, b, ks):
        for k in ks:
            pass_on(full, b, behind(k))

    half = n // groups
    first, second = order[:half], order[half:]
    for copy in t_copies:
        copy.wait()
    pick(slot_lane, send_e)
    pl.semaphore_wait(barrier, n + 1)
    dispatch(send_e, full_e, ae, first[1:])
    full_e[t, me] = send_e[me]
    moved = pos_lane
    for e in range(n):
        moved = moved + jnp.where(te[...] == e, (partner[e] * cap).astype(F32), 0.0)
    pick(moved, send_p)
    full_p[t, me] = send_p[me]
    if WAVE:
        sent(send_e, ae, first[1:])
    dispatch(send_e, full_e, ae, second)
    if not WAVE:
        sent(send_e, ae, first[1:])

    slices = (t, ctr, sib, far)

    def compute(h):
        ks = order[h * per : (h + 1) * per]
        for k in ks:
            got_sibling(full_e, be, behind(k))
        gate = jnp.zeros((per * cap, units), F32)
        upward = jnp.zeros((per * cap, units), F32)
        hidden_grad = jnp.zeros((per * cap, units), F32)
        for q in range(4):
            x_q = jnp.concatenate([full_e[q, behind(k), 0] for k in ks], axis=0)
            g_q = jnp.concatenate([full_e[q, behind(k), 1] for k in ks], axis=0)
            gate = gate + contract_last(x_q, w_v[0, q])
            upward = upward + contract_last(x_q, w_v[1, q])
            hidden_grad = hidden_grad + contract_last(g_q, w_v[2, q])
        gate_term, up_term, hidden = expert_terms(gate, upward, hidden_grad)
        for j, k in enumerate(ks):
            cut = slice(j * cap, (j + 1) * cap)
            terms[behind(k), :, 0:units] = gate_term[cut]
            terms[behind(k), :, units : 2 * units] = up_term[cut]
            terms[behind(k), :, 2 * units : 3 * units] = hidden[cut]
            if terms.shape[2] > 3 * units:
                terms[behind(k), :, 3 * units :] = jnp.zeros((cap, terms.shape[2] - 3 * units), BF16)
        for k in ks:
            s = behind(k)
            if k == 0:
                mid[me] = terms[me]
            else:
                remote(terms.at[s], mid.at[me], e1.at[0, s], e1.at[1, me], {"ep": s}).start()
        for i in (2, 3):
            q = slices[i]
            c1s[h, i - 2] = (
                jnp.dot(gate_term, w_v[0, q], preferred_element_type=F32)
                + jnp.dot(up_term, w_v[1, q], preferred_element_type=F32)
            ).astype(BF16)
        remote(c1s.at[h], c1r.at[h], c1.at[0, h], c1.at[1, h], {"tp": sib}).start()
        for i in (0, 1):
            q = slices[i]
            keep[h, i] = jnp.dot(gate_term, w_v[0, q], preferred_element_type=F32) + jnp.dot(
                up_term, w_v[1, q], preferred_element_type=F32
            )

    def sum_siblings(h):
        remote(c1s.at[h], c1r.at[h], c1.at[0, h], c1.at[1, h], {"tp": sib}).wait_recv()
        c2s[h] = (keep[h, 1] + c1r[h, 1].astype(F32)).astype(BF16)
        remote(c2s.at[h], c2r.at[h], c2.at[0, h], c2.at[1, h], {"tp": ctr}).start()

    def send_back(h):
        remote(c2s.at[h], c2r.at[h], c2.at[0, h], c2.at[1, h], {"tp": ctr}).wait_recv()
        total = (keep[h, 0] + c1r[h, 0].astype(F32) + c2r[h].astype(F32)).astype(BF16)
        shares[h * per : (h + 1) * per] = total.reshape(per, cap, width)
        for i in range(h * per, (h + 1) * per):
            s = behind(order[i])
            if i == 0:
                ret[me] = shares[0]
            else:
                remote(shares.at[i], ret.at[me], dd.at[0, s], dd.at[1, me], {"ep": s}).start()

    def weights_ready():
        for copy in w_copies:
            copy.wait()

    take(full_e, ae, be, first)
    relay(full_e, be, first)
    weights_ready()
    if G0:
        compute(0)
        take(full_e, ae, be, second)
        dispatch(send_p, full_p, ap, order[1:])
    else:
        take(full_e, ae, be, second)
        dispatch(send_p, full_p, ap, order[1:])
        compute(0)
    sum_siblings(0)
    relay(full_e, be, second)
    if BP == 0:
        compute(1)
        send_back(0)
        sum_siblings(1)
        take(full_p, ap, bp, order)
        send_back(1)
    elif BP == 1:
        compute(1)
        send_back(0)
        sum_siblings(1)
        send_back(1)
        take(full_p, ap, bp, order)
    elif BP == 2:
        send_back(0)
        compute(1)
        sum_siblings(1)
        take(full_p, ap, bp, order)
        send_back(1)
    elif BP == 3:
        compute(1)
        send_back(0)
        sum_siblings(1)
        take(full_p, ap, bp, first)
        send_back(1)
        take(full_p, ap, bp, second)

    def first_hop(k, carry):
        s = ahead(k)
        remote(mid.at[s], mid.at[s], e1.at[0, s], e1.at[1, s], {"ep": s}).wait_recv()
        return carry
    lax.fori_loop(1, n, first_hop, 0)

    def second_hop(k, carry):
        d = ahead(k)
        send2[d] = mid[partner[d]]
        remote(send2.at[d], terms_p.at[me], e2.at[0, d], e2.at[1, me], {"ep": d}).start()
        return carry
    lax.fori_loop(1, n, second_hop, 0)
    terms_p[me] = mid[partner[me]]
    relay(full_p, bp, order)

    def returned(k, carry):
        s = behind(k)
        remote(ret.at[s], ret.at[s], dd.at[0, s], dd.at[1, s], {"ep": s}).wait_recv()
        remote(terms_p.at[s], terms_p.at[s], e2.at[0, s], e2.at[1, s], {"ep": s}).wait_recv()
        return carry
    lax.fori_loop(1, n, returned, 0)

    def gathered(k, carry):
        got_sibling(full_p, bp, behind(k))
        return carry
    lax.fori_loop(0, n, gathered, 0)

    sent(send_e, ae, second)

    def drain(k, carry):
        s = ahead(k)
        remote(send_p.at[s], send_p.at[s], ap.at[0, s], ap.at[1, s], {"ep": s}).wait_send()
        remote(terms.at[s], terms.at[s], e1.at[0, s], e1.at[1, s], {"ep": s}).wait_send()
        remote(send2.at[s], send2.at[s], e2.at[0, s], e2.at[1, s], {"ep": s}).wait_send()
        remote(ret.at[s], ret.at[s], dd.at[0, s], dd.at[1, s], {"ep": s}).wait_send()
        return carry
    lax.fori_loop(1, n, drain, 0)

    def drain_tp(s, carry):
        for full, b in ((full_e, be), (full_p, bp)):
            for i, (q, other) in enumerate(((t, sib), (t, ctr), (ctr, sib))):
                remote(full.at[q, s], full.at[q, s], b.at[i, s], b.at[3 + i, s], {"tp": other}).wait_send()
        return carry
    lax.fori_loop(0, n, drain_tp, 0)
    for h in range(groups):
        remote(c1s.at[h], c1r.at[h], c1.at[0, h], c1.at[1, h], {"tp": sib}).wait_send()
        remote(c2s.at[h], c2r.at[h], c2.at[0, h], c2.at[1, h], {"tp": ctr}).wait_send()


def kernel_body(tokens, cotangent, token_expert, partner, gate_weight, up_weight, down_weight):
    n = lax.axis_size("ep")
    rows, width = tokens.shape
    _, units, features = gate_weight.shape
    cap = capacity_of(rows, n)
    groups = 2
    per = n // groups
    padded = -(-3 * units // 128) * 128
    dma = pltpu.SemaphoreType.DMA
    vmem = pl.BlockSpec(memory_space=pltpu.VMEM)
    hbm = pl.BlockSpec(memory_space=pltpu.HBM)
    grad = jax.ShapeDtypeStruct((1, units, features), BF16)
    te = token_expert.reshape(1, rows)
    in_hbm = [
        pltpu.with_memory_space_constraint(a, pltpu.HBM)
        for a in (tokens, cotangent, gate_weight, up_weight, down_weight)
    ]
    kept, terms, back = pl.pallas_call(
        functools.partial(swap_kernel, n, cap, groups),
        out_shape=(
            jax.ShapeDtypeStruct((4, n, 2, cap, width), BF16),
            jax.ShapeDtypeStruct((n, cap, padded), BF16),
            jax.ShapeDtypeStruct((n, cap, width), BF16),
        ),
        in_specs=[pl.BlockSpec(memory_space=pltpu.SMEM), vmem] + [hbm] * 5,
        out_specs=(vmem, vmem, vmem),
        scratch_shapes=[
            pltpu.VMEM((rows, width), BF16),
            pltpu.VMEM((rows, width), BF16),
            pltpu.VMEM((3, 4, units, width), BF16),
            pltpu.VMEM((n, 2, cap, width), BF16),
            pltpu.VMEM((n, 2, cap, width), BF16),
            pltpu.VMEM((4, n, 2, cap, width), BF16),
            pltpu.VMEM((n, cap, padded), BF16),
            pltpu.VMEM((n, cap, padded), BF16),
            pltpu.VMEM((n, cap, padded), BF16),
            pltpu.VMEM((groups, 2, per * cap, width), F32),
            pltpu.VMEM((groups, 2, per * cap, width), BF16),
            pltpu.VMEM((groups, 2, per * cap, width), BF16),
            pltpu.VMEM((groups, per * cap, width), BF16),
            pltpu.VMEM((groups, per * cap, width), BF16),
            pltpu.VMEM((n, cap, width), BF16),
            dma((2,)),
            dma((3, 4)),
            dma((2, n)),
            dma((2, n)),
            dma((6, n)),
            dma((6, n)),
            dma((2, n)),
            dma((2, n)),
            dma((2, groups)),
            dma((2, groups)),
            dma((2, n)),
        ],
        compiler_params=pltpu.CompilerParams(
            collective_id=0, has_side_effects=True, vmem_limit_bytes=48 * 2**20
        ),
        cost_estimate=pl.CostEstimate(
            flops=10 * n * cap * units * features,
            bytes_accessed=6 * units * features + 4 * rows * width,
            transcendentals=n * cap * units,
        ),
    )(partner, te, *in_hbm)
    return pl.pallas_call(
        functools.partial(result_kernel, cap),
        out_shape=(jax.ShapeDtypeStruct((rows, width), BF16), grad, grad, grad),
        in_specs=[vmem] * 4,
        out_specs=(hbm,) * 4,
        scratch_shapes=[
            pltpu.VMEM((rows, width), BF16),
            pltpu.VMEM((12, units, width), BF16),
            dma((13,)),
        ],
        compiler_params=pltpu.CompilerParams(vmem_limit_bytes=32 * 2**20),
        cost_estimate=pl.CostEstimate(
            flops=6 * n * cap * units * features,
            bytes_accessed=6 * units * features + 2 * rows * width,
            transcendentals=0,
        ),
    )(te, kept, terms, back)


def body(tokens, cotangent, token_expert, partner, gate_weight, up_weight, down_weight):
    n, ranks = lax.axis_size("ep"), lax.axis_size("tp")
    rows, width = tokens.shape
    cap = capacity_of(rows, n)
    tiled = cap % 16 == 0 and rows % 128 == 0 and width % 128 == 0 and n % 2 == 0 and ranks == 4
    fits = 32 * n * cap * width <= 8 * 2**20
    chosen = kernel_body if tiled and fits else plain_body
    return chosen(tokens, cotangent, token_expert, partner, gate_weight, up_weight, down_weight)


def solution(mesh):
    in_specs = (
        P("ep", "tp"),
        P("ep", "tp"),
        P("ep"),
        P(),
        P("ep", "tp", None),
        P("ep", "tp", None),
        P("ep", "tp", None),
    )
    out_specs = (P("ep", "tp"), P("ep", "tp", None), P("ep", "tp", None), P("ep", "tp", None))
    return jax.shard_map(body, mesh=mesh, in_specs=in_specs, out_specs=out_specs, check_vma=False)
```

```python
import functools

import jax
import jax.numpy as jnp
from jax import lax
from jax.experimental import pallas as pl
from jax.experimental.pallas import tpu as pltpu
from jax.sharding import PartitionSpec as P

F32 = jnp.float32
BF16 = jnp.bfloat16


def contract_last(left, right):
    return lax.dot_general(left, right, (((1,), (1,)), ((), ())), preferred_element_type=F32)


def contract_first(left, right):
    return lax.dot_general(left, right, (((0,), (0,)), ((), ())), preferred_element_type=F32)


def expert_terms(gate, upward, hidden_grad):
    sigmoid_gate = jax.nn.sigmoid(gate)
    activated = gate * sigmoid_gate
    hidden = (activated * upward).astype(BF16)
    up_term = (hidden_grad * activated).astype(BF16)
    gate_term = (hidden_grad * upward * sigmoid_gate * (1.0 + gate * (1.0 - sigmoid_gate))).astype(BF16)
    return gate_term, up_term, hidden


def capacity_of(rows, devices):
    return max(2, (2 * rows + devices - 1) // devices)


def relocate(arrays, partner):
    devices = lax.axis_size("ep")
    pieces = tuple((matrix.reshape(devices, -1) for matrix in arrays))
    spread = lax.all_to_all(pieces, "ep", split_axis=0, concat_axis=0, tiled=True)
    chosen = tuple((jnp.take(piece, partner, axis=0) for piece in spread))
    returned = lax.all_to_all(chosen, "ep", split_axis=0, concat_axis=0, tiled=True)
    return tuple((piece.reshape(matrix.shape) for piece, matrix in zip(returned, arrays)))


def plain_body(tokens, cotangent, token_expert, partner, gate_weight, up_weight, down_weight):
    devices = lax.axis_size("ep")
    row_count = tokens.shape[0]
    capacity = capacity_of(row_count, devices)
    gate_weight, up_weight, down_weight = relocate((gate_weight, up_weight, down_weight), partner)
    owners = jnp.take(partner, token_expert, axis=0)
    same_owner = owners[:, None] == owners[None, :]
    earlier = jnp.arange(row_count)[:, None] > jnp.arange(row_count)[None, :]
    position = jnp.sum((same_owner & earlier).astype(jnp.int32), axis=1)
    slot_of = owners * capacity + position
    one_hot = (slot_of[None, :] == jnp.arange(devices * capacity)[:, None]).astype(BF16)
    send_x = jnp.dot(one_hot, tokens, preferred_element_type=F32).astype(BF16)
    send_g = jnp.dot(one_hot, cotangent, preferred_element_type=F32).astype(BF16)
    received_x = lax.all_to_all(send_x, "ep", split_axis=0, concat_axis=0, tiled=True)
    received_g = lax.all_to_all(send_g, "ep", split_axis=0, concat_axis=0, tiled=True)
    full_x = lax.all_gather(received_x, "tp", axis=1, tiled=True)
    full_g = lax.all_gather(received_g, "tp", axis=1, tiled=True)
    w_gate, w_up, w_down = gate_weight[0], up_weight[0], down_weight[0]
    gate_term, up_term, hidden = expert_terms(
        contract_last(full_x, w_gate), contract_last(full_x, w_up), contract_last(full_g, w_down)
    )
    partial_value = jnp.dot(gate_term, w_gate, preferred_element_type=F32) + jnp.dot(
        up_term, w_up, preferred_element_type=F32
    )
    grad_gate = contract_first(gate_term, full_x).astype(BF16)[None]
    grad_up = contract_first(up_term, full_x).astype(BF16)[None]
    grad_down = contract_first(hidden, full_g).astype(BF16)[None]
    share = lax.psum_scatter(partial_value, "tp", scatter_dimension=1, tiled=True).astype(BF16)
    coming_back = lax.all_to_all(share, "ep", split_axis=0, concat_axis=0, tiled=True)
    token_grad = contract_first(one_hot, coming_back).astype(BF16)
    return (token_grad, grad_gate, grad_up, grad_down)


def remote(src, dst, send, recv, device):
    return pltpu.make_async_remote_copy(
        src_ref=src, dst_ref=dst, send_sem=send, recv_sem=recv,
        device_id=device, device_id_type=pl.DeviceIdType.MESH,
    )


def slots_of(te, cap):
    rows = te.shape[1]
    te_lane = jnp.broadcast_to(te.astype(F32), (rows, rows))
    te_sub = te_lane.T
    at0 = lax.broadcasted_iota(jnp.int32, (rows, rows), 0)
    at1 = lax.broadcasted_iota(jnp.int32, (rows, rows), 1)
    same = te_lane == te_sub
    pos_lane = jnp.sum(jnp.where(same & (at0 < at1), 1.0, 0.0), axis=0, keepdims=True)
    pos_sub = jnp.sum(jnp.where(same & (at1 < at0), 1.0, 0.0), axis=1, keepdims=True)
    return te.astype(F32) * float(cap) + pos_lane, pos_lane, te_sub[:, :1] * float(cap) + pos_sub


WAVE, G0, BP = False, 0, 2


def result_kernel(
    cap, te, full_p, terms_p, ret, tg_out, gg_out, gu_out, gd_out, tg_v, g_v, out_sem
):
    n, _, padded = terms_p.shape
    rows, width = tg_v.shape
    units = g_v.shape[1]
    slots = n * cap
    turned = terms_p[...].reshape(slots, padded).astype(F32).T.astype(BF16)
    copies = []
    for q in range(4):
        columns = pl.ds(q * width, width)
        x_q = full_p[q, :, 0].reshape(slots, width)
        g_q = full_p[q, :, 1].reshape(slots, width)
        for i, (out, by) in enumerate(((gg_out, x_q), (gu_out, x_q), (gd_out, g_q))):
            part = turned[i * units : (i + 1) * units]
            g_v[3 * q + i] = jnp.dot(part, by, preferred_element_type=F32).astype(BF16)
            copy = pltpu.make_async_copy(g_v.at[3 * q + i], out.at[0, :, columns], out_sem.at[3 * q + i])
            copy.start()
            copies.append(copy)
    _, _, slot_sub = slots_of(te[...], cap)
    across = lax.broadcasted_iota(jnp.int32, (rows, slots), 1).astype(F32)
    home = jnp.where(across == slot_sub, 1.0, 0.0).astype(BF16)
    tg_v[...] = jnp.dot(home, ret[...].reshape(slots, width), preferred_element_type=F32).astype(BF16)
    copy = pltpu.make_async_copy(tg_v, tg_out, out_sem.at[12])
    copy.start()
    for done in copies + [copy]:
        done.wait()


def swap_kernel(
    n, cap, groups,
    partner_in, te_in, tok_in, cot_in, wg_in, wu_in, wd_in,
    full_p, terms_p, ret,
    partner, te, tok, cot, w_v, send_e, send_p, full_e, terms, mid, send2,
    keep, c1s, c1r, c2s, c2r, shares,
    t_sem, w_sem, ae, ap, be, bp, e1, e2, c1, c2, dd,
):
    rows, width = tok.shape
    units = wg_in.shape[1]
    per = n // groups
    me = lax.axis_index("ep")
    t = lax.axis_index("tp")
    sib = t + 1 - 2 * lax.rem(t, 2)
    ctr = lax.rem(t + 2, 4)
    far = lax.rem(sib + 2, 4)
    order = [i + j for i in range(n // 2) for j in (0, n // 2)]
    ahead = lambda k: lax.rem(me + k, n)
    behind = lambda k: lax.rem(me + n - k, n)

    t_copies = [
        pltpu.make_async_copy(a, v, t_sem.at[i]) for i, (a, v) in enumerate(((te_in, te), (partner_in, partner), (tok_in, tok), (cot_in, cot)))
    ]
    for copy in t_copies:
        copy.start()
    barrier = pltpu.get_barrier_semaphore()

    def greet(k, carry):
        pl.semaphore_signal(barrier, inc=1, device_id={"ep": ahead(k)}, device_id_type=pl.DeviceIdType.MESH)
        return carry

    lax.fori_loop(1, n, greet, 0)
    for other in (sib, ctr):
        pl.semaphore_signal(barrier, inc=1, device_id={"tp": other}, device_id_type=pl.DeviceIdType.MESH)

    w_copies = [
        pltpu.make_async_copy(
            w.at[0, :, pl.ds(q * width, width)], w_v.at[i, q], w_sem.at[i, q]
        )
        for i, w in enumerate((wg_in, wu_in, wd_in))
        for q in range(4)
    ]
    for copy in w_copies:
        copy.start()

    for copy in t_copies:
        copy.wait()
    slot_lane, pos_lane, _ = slots_of(te[...], cap)
    slots = n * cap
    down = lax.broadcasted_iota(jnp.int32, (slots, rows), 0).astype(F32)

    def pick(slot, send):
        hot = jnp.where(down == slot, 1.0, 0.0).astype(BF16)
        for i, source in enumerate((tok, cot)):
            rows_of = jnp.dot(hot, source[...], preferred_element_type=F32).astype(BF16)
            send[:, i] = rows_of.reshape(n, cap, width)

    def dispatch(send, full, sem, ks):
        for k in ks:
            to = ahead(k)
            remote(send.at[to], full.at[t, me], sem.at[0, to], sem.at[1, me], {"ep": to}).start()

    def sent(send, sem, ks):
        for k in ks:
            to = ahead(k)
            remote(send.at[to], send.at[to], sem.at[0, to], sem.at[1, to], {"ep": to}).wait_send()

    def share_own(full, b, s):
        remote(full.at[t, s], full.at[t, s], b.at[1, s], b.at[4, s], {"tp": ctr}).start()
        remote(full.at[t, s], full.at[t, s], b.at[0, s], b.at[3, s], {"tp": sib}).start()

    def got_own(full, a, s, k):
        remote(full.at[t, s], full.at[t, s], a.at[0, s], a.at[1, s], {"ep": s}).wait_recv()

    def pass_on(full, b, s):
        remote(full.at[ctr, s], full.at[ctr, s], b.at[1, s], b.at[4, s], {"tp": ctr}).wait_recv()
        remote(full.at[ctr, s], full.at[ctr, s], b.at[2, s], b.at[5, s], {"tp": sib}).start()

    def got_sibling(full, b, s):
        remote(full.at[sib, s], full.at[sib, s], b.at[0, s], b.at[3, s], {"tp": sib}).wait_recv()
        remote(full.at[far, s], full.at[far, s], b.at[2, s], b.at[5, s], {"tp": sib}).wait_recv()

    def take(full, a, b, ks):
        for k in ks:
            s = behind(k)
            if k:
                got_own(full, a, s, k)
            share_own(full, b, s)

    def relay(full, b, ks):
        for k in ks:
            pass_on(full, b, behind(k))

    half = n // groups
    first, second = order[:half], order[half:]
    pick(slot_lane, send_e)
    pl.semaphore_wait(barrier, n + 1)
    dispatch(send_e, full_e, ae, first[1:])
    full_e[t, me] = send_e[me]
    moved = pos_lane
    for e in range(n):
        moved = moved + jnp.where(te[...] == e, (partner[e] * cap).astype(F32), 0.0)
    pick(moved, send_p)
    full_p[t, me] = send_p[me]
    if WAVE:
        sent(send_e, ae, first[1:])
    dispatch(send_e, full_e, ae, second)
    if not WAVE:
        sent(send_e, ae, first[1:])

    slices = (t, ctr, sib, far)

    def compute(h):
        ks = order[h * per : (h + 1) * per]
        for k in ks:
            got_sibling(full_e, be, behind(k))
        gate = jnp.zeros((per * cap, units), F32)
        upward = jnp.zeros((per * cap, units), F32)
        hidden_grad = jnp.zeros((per * cap, units), F32)
        for q in range(4):
            x_q = jnp.concatenate([full_e[q, behind(k), 0] for k in ks], axis=0)
            g_q = jnp.concatenate([full_e[q, behind(k), 1] for k in ks], axis=0)
            gate = gate + contract_last(x_q, w_v[0, q])
            upward = upward + contract_last(x_q, w_v[1, q])
            hidden_grad = hidden_grad + contract_last(g_q, w_v[2, q])
        gate_term, up_term, hidden = expert_terms(gate, upward, hidden_grad)
        for j, k in enumerate(ks):
            cut = slice(j * cap, (j + 1) * cap)
            terms[behind(k), :, 0:units] = gate_term[cut]
            terms[behind(k), :, units : 2 * units] = up_term[cut]
            terms[behind(k), :, 2 * units : 3 * units] = hidden[cut]
            if terms.shape[2] > 3 * units:
                terms[behind(k), :, 3 * units :] = jnp.zeros((cap, terms.shape[2] - 3 * units), BF16)
        for k in ks:
            s = behind(k)
            if k == 0:
                mid[me] = terms[me]
            else:
                remote(terms.at[s], mid.at[me], e1.at[0, s], e1.at[1, me], {"ep": s}).start()
        for i in (2, 3):
            q = slices[i]
            c1s[h, i - 2] = (
                jnp.dot(gate_term, w_v[0, q], preferred_element_type=F32)
                + jnp.dot(up_term, w_v[1, q], preferred_element_type=F32)
            ).astype(BF16)
        remote(c1s.at[h], c1r.at[h], c1.at[0, h], c1.at[1, h], {"tp": sib}).start()
        for i in (0, 1):
            q = slices[i]
            keep[h, i] = jnp.dot(gate_term, w_v[0, q], preferred_element_type=F32) + jnp.dot(
                up_term, w_v[1, q], preferred_element_type=F32
            )

    def sum_siblings(h):
        remote(c1s.at[h], c1r.at[h], c1.at[0, h], c1.at[1, h], {"tp": sib}).wait_recv()
        c2s[h] = (keep[h, 1] + c1r[h, 1].astype(F32)).astype(BF16)
        remote(c2s.at[h], c2r.at[h], c2.at[0, h], c2.at[1, h], {"tp": ctr}).start()

    def send_back(h):
        remote(c2s.at[h], c2r.at[h], c2.at[0, h], c2.at[1, h], {"tp": ctr}).wait_recv()
        total = (keep[h, 0] + c1r[h, 0].astype(F32) + c2r[h].astype(F32)).astype(BF16)
        shares[h * per : (h + 1) * per] = total.reshape(per, cap, width)
        for i in range(h * per, (h + 1) * per):
            s = behind(order[i])
            if i == 0:
                ret[me] = shares[0]
            else:
                remote(shares.at[i], ret.at[me], dd.at[0, s], dd.at[1, me], {"ep": s}).start()

    def weights_ready():
        for copy in w_copies:
            copy.wait()

    take(full_e, ae, be, first)
    if G0 != 0:
        relay(full_e, be, first)
    weights_ready()
    if G0 == 1:
        compute(0)
        take(full_e, ae, be, second)
        dispatch(send_p, full_p, ap, order[1:])
    elif G0 == 0:
        take(full_e, ae, be, second)
        dispatch(send_p, full_p, ap, order[1:])
        relay(full_e, be, first)
        compute(0)
    else:
        dispatch(send_p, full_p, ap, first[1:])
        take(full_e, ae, be, second)
        dispatch(send_p, full_p, ap, second)
        compute(0)
    sum_siblings(0)
    relay(full_e, be, second)
    if BP == 6:
        take(full_p, ap, bp, first)
        compute(1)
        send_back(0)
        sum_siblings(1)
        take(full_p, ap, bp, second)
        send_back(1)
    elif BP == 7:
        compute(1)
        take(full_p, ap, bp, order)
        send_back(0)
        sum_siblings(1)
        send_back(1)
    elif BP == 0:
        compute(1)
        send_back(0)
        sum_siblings(1)
        take(full_p, ap, bp, order)
        send_back(1)
    elif BP == 1:
        compute(1)
        send_back(0)
        sum_siblings(1)
        send_back(1)
        take(full_p, ap, bp, order)
    elif BP == 2:
        send_back(0)
        compute(1)
        sum_siblings(1)
        take(full_p, ap, bp, order)
        send_back(1)
    elif BP == 3:
        compute(1)
        send_back(0)
        sum_siblings(1)
        take(full_p, ap, bp, first)
        send_back(1)
        take(full_p, ap, bp, second)
    else:
        compute(1)
        send_back(0)
        sum_siblings(1)
        send_back(1)

    def first_hop(k, carry):
        s = ahead(k)
        remote(mid.at[s], mid.at[s], e1.at[0, s], e1.at[1, s], {"ep": s}).wait_recv()
        return carry
    lax.fori_loop(1, n, first_hop, 0)
    if BP == 5:
        take(full_p, ap, bp, order)

    def second_hop(k, carry):
        d = ahead(k)
        send2[d] = mid[partner[d]]
        remote(send2.at[d], terms_p.at[me], e2.at[0, d], e2.at[1, me], {"ep": d}).start()
        return carry
    lax.fori_loop(1, n, second_hop, 0)
    terms_p[me] = mid[partner[me]]
    if BP == 4:
        take(full_p, ap, bp, order)
    relay(full_p, bp, order)

    def returned(k, carry):
        s = behind(k)
        remote(ret.at[s], ret.at[s], dd.at[0, s], dd.at[1, s], {"ep": s}).wait_recv()
        remote(terms_p.at[s], terms_p.at[s], e2.at[0, s], e2.at[1, s], {"ep": s}).wait_recv()
        return carry
    lax.fori_loop(1, n, returned, 0)

    def gathered(k, carry):
        got_sibling(full_p, bp, behind(k))
        return carry
    lax.fori_loop(0, n, gathered, 0)

    sent(send_e, ae, second)

    def drain(k, carry):
        s = ahead(k)
        remote(send_p.at[s], send_p.at[s], ap.at[0, s], ap.at[1, s], {"ep": s}).wait_send()
        remote(terms.at[s], terms.at[s], e1.at[0, s], e1.at[1, s], {"ep": s}).wait_send()
        remote(send2.at[s], send2.at[s], e2.at[0, s], e2.at[1, s], {"ep": s}).wait_send()
        remote(ret.at[s], ret.at[s], dd.at[0, s], dd.at[1, s], {"ep": s}).wait_send()
        return carry
    lax.fori_loop(1, n, drain, 0)

    def drain_tp(s, carry):
        for full, b in ((full_e, be), (full_p, bp)):
            for i, (q, other) in enumerate(((t, sib), (t, ctr), (ctr, sib))):
                remote(full.at[q, s], full.at[q, s], b.at[i, s], b.at[3 + i, s], {"tp": other}).wait_send()
        return carry
    lax.fori_loop(0, n, drain_tp, 0)
    for h in range(groups):
        remote(c1s.at[h], c1r.at[h], c1.at[0, h], c1.at[1, h], {"tp": sib}).wait_send()
        remote(c2s.at[h], c2r.at[h], c2.at[0, h], c2.at[1, h], {"tp": ctr}).wait_send()


def kernel_body(tokens, cotangent, token_expert, partner, gate_weight, up_weight, down_weight):
    n = lax.axis_size("ep")
    rows, width = tokens.shape
    _, units, features = gate_weight.shape
    cap = capacity_of(rows, n)
    groups = 2
    per = n // groups
    padded = -(-3 * units // 128) * 128
    dma = pltpu.SemaphoreType.DMA
    vmem = pl.BlockSpec(memory_space=pltpu.VMEM)
    hbm = pl.BlockSpec(memory_space=pltpu.HBM)
    grad = jax.ShapeDtypeStruct((1, units, features), BF16)
    te = token_expert.reshape(1, rows)
    in_hbm = [
        pltpu.with_memory_space_constraint(a, pltpu.HBM)
        for a in (partner, te, tokens, cotangent, gate_weight, up_weight, down_weight)
    ]
    kept, terms, back = pl.pallas_call(
        functools.partial(swap_kernel, n, cap, groups),
        out_shape=(
            jax.ShapeDtypeStruct((4, n, 2, cap, width), BF16),
            jax.ShapeDtypeStruct((n, cap, padded), BF16),
            jax.ShapeDtypeStruct((n, cap, width), BF16),
        ),
        in_specs=[hbm] * 7,
        out_specs=(vmem, vmem, vmem),
        scratch_shapes=[
            pltpu.SMEM((n,), jnp.int32),
            pltpu.VMEM((1, rows), jnp.int32),
            pltpu.VMEM((rows, width), BF16),
            pltpu.VMEM((rows, width), BF16),
            pltpu.VMEM((3, 4, units, width), BF16),
            pltpu.VMEM((n, 2, cap, width), BF16),
            pltpu.VMEM((n, 2, cap, width), BF16),
            pltpu.VMEM((4, n, 2, cap, width), BF16),
            pltpu.VMEM((n, cap, padded), BF16),
            pltpu.VMEM((n, cap, padded), BF16),
            pltpu.VMEM((n, cap, padded), BF16),
            pltpu.VMEM((groups, 2, per * cap, width), F32),
            pltpu.VMEM((groups, 2, per * cap, width), BF16),
            pltpu.VMEM((groups, 2, per * cap, width), BF16),
            pltpu.VMEM((groups, per * cap, width), BF16),
            pltpu.VMEM((groups, per * cap, width), BF16),
            pltpu.VMEM((n, cap, width), BF16),
            dma((4,)),
            dma((3, 4)),
            dma((2, n)),
            dma((2, n)),
            dma((6, n)),
            dma((6, n)),
            dma((2, n)),
            dma((2, n)),
            dma((2, groups)),
            dma((2, groups)),
            dma((2, n)),
        ],
        compiler_params=pltpu.CompilerParams(
            collective_id=0, has_side_effects=True, vmem_limit_bytes=48 * 2**20
        ),
        cost_estimate=pl.CostEstimate(
            flops=10 * n * cap * units * features,
            bytes_accessed=6 * units * features + 4 * rows * width,
            transcendentals=n * cap * units,
        ),
    )(*in_hbm)
    return pl.pallas_call(
        functools.partial(result_kernel, cap),
        out_shape=(jax.ShapeDtypeStruct((rows, width), BF16), grad, grad, grad),
        in_specs=[vmem] * 4,
        out_specs=(hbm,) * 4,
        scratch_shapes=[
            pltpu.VMEM((rows, width), BF16),
            pltpu.VMEM((12, units, width), BF16),
            dma((13,)),
        ],
        compiler_params=pltpu.CompilerParams(vmem_limit_bytes=32 * 2**20),
        cost_estimate=pl.CostEstimate(
            flops=6 * n * cap * units * features,
            bytes_accessed=6 * units * features + 2 * rows * width,
            transcendentals=0,
        ),
    )(te, kept, terms, back)


def body(tokens, cotangent, token_expert, partner, gate_weight, up_weight, down_weight):
    n, ranks = lax.axis_size("ep"), lax.axis_size("tp")
    rows, width = tokens.shape
    cap = capacity_of(rows, n)
    tiled = cap % 16 == 0 and rows % 128 == 0 and width % 128 == 0 and n % 2 == 0 and ranks == 4
    fits = 32 * n * cap * width <= 8 * 2**20
    chosen = kernel_body if tiled and fits else plain_body
    return chosen(tokens, cotangent, token_expert, partner, gate_weight, up_weight, down_weight)


def solution(mesh):
    in_specs = (
        P("ep", "tp"),
        P("ep", "tp"),
        P("ep"),
        P(),
        P("ep", "tp", None),
        P("ep", "tp", None),
        P("ep", "tp", None),
    )
    out_specs = (P("ep", "tp"), P("ep", "tp", None), P("ep", "tp", None), P("ep", "tp", None))
    return jax.shard_map(body, mesh=mesh, in_specs=in_specs, out_specs=out_specs, check_vma=False)
```
